32 devices in a mesh: gx: 4 (over x, core), gy: 8 (over z, y).
Axes of the slice: x: 2, y: 2, z: 4, core: 2. Of those that a mesh axis runs over, the one named last changes fastest.
Arguments:
- features: bfloat16 [4, 8, 2, 96, 4096], P('gx', 'gy'), may hold values from -6 to 6
- grad_out: bfloat16 [4, 8, 2, 96, 4096], P('gx', 'gy'), may hold values from -6 to 6
- weight: bfloat16 [96, 2592], replicated, may hold values from -0.125 to 0.125
- active: int32 [4, 8, 2], P('gx', 'gy'), may hold values from 0 to 1, as said below
Outputs:
- out: bfloat16 [4, 8, 2, 96, 4096], P('gx', 'gy')
- grad_in: bfloat16 [4, 8, 2, 96, 4096], P('gx', 'gy')
- grad_weight: float32 [248832], P(('gx', 'gy'))
The draws below stay inside these ranges and needn't reach their ends.
Inputs may be any that keep to these rules, and one draw needn't show every extreme that they name: The two columns with the same gx index and gy indices 2m and 2m + 1 hold exactly 2 active bricks together, so a column holds 0 to 2 of them; some column holds 2 in every draw.
All inputs are finite; a program needn't handle non-finite values.
Results may differ from the reference program's by a relative error of at most 0.001.
Values may be sent and summed in bfloat16 or wider, within the bound.
A program may use at most 128 MiB of HBM per device.

```python
import math
import jax
import jax.numpy as jnp
from jax import lax

C = 96
EDGE = 16
LEVELS = 2
COLS_X = 4
COLS_Y = 8
VOX = 4096
KW = 248832


def draw_active(key, part):
    split_key = jax.random.fold_in(key, 11)
    splits = jax.random.randint(split_key, (COLS_X, COLS_Y // 2), 0, LEVELS + 1)
    pick_x = jax.random.randint(jax.random.fold_in(key, 12), (), 0, COLS_X)
    pick_y = jax.random.randint(jax.random.fold_in(key, 13), (), 0, COLS_Y // 2)
    full_side = LEVELS * jax.random.randint(jax.random.fold_in(key, 14), (), 0, 2)
    splits = splits.at[pick_x, pick_y].set(full_side)
    counts = jnp.stack([splits, LEVELS - splits], axis=-1).reshape(COLS_X, COLS_Y)
    scores = jax.random.randint(jax.random.fold_in(key, 15), (COLS_X, COLS_Y, LEVELS), 0, 1 << 20)
    scores = scores * LEVELS + jnp.arange(LEVELS, dtype=jnp.int32)
    ranks = jnp.argsort(jnp.argsort(scores, axis=-1), axis=-1)
    return (ranks < counts[..., None]).astype(jnp.int32)


def steps_of(own_key, dims, split, smallest, top_value):
    def one(dim, shards_of):
        heights = jax.random.uniform(jax.random.fold_in(jax.random.fold_in(own_key, 6), dim), (shards_of,), jnp.float32, smallest / len(split), top_value / len(split))
        return jnp.repeat(jnp.exp(heights), dims[dim] // shards_of).reshape((-1,) + (1,) * (len(dims) - dim - 1))

    level = one(*split[0])
    for cut in split[1:]:
        level = level * one(*cut)
    return level


def centred(rng, dims, deviation, reach, shards=(), kind=jnp.bfloat16):
    values = deviation * jax.random.normal(rng, dims, jnp.float32)
    if shards:
        values = values * steps_of(rng, dims, shards, -0.22, 0.18)
    return jnp.clip(values, -reach, reach).astype(kind)


def setup_inputs(seed: int = 0) -> dict:
    streams_of = jax.random.split(jax.random.key(seed), 5)
    return {
        "features": centred(streams_of[0], (COLS_X, COLS_Y, LEVELS, C, VOX), 1.0, 6.0, ((0, 4), (1, 8))),
        "grad_out": centred(streams_of[1], (COLS_X, COLS_Y, LEVELS, C, VOX), 1.0, 6.0, ((0, 4), (1, 8))),
        "weight": centred(streams_of[2], (C, 27 * C), (27 * C) ** -0.5, 0.125),
        "active": draw_active(jax.random.fold_in(streams_of[4], 71), 0),
    }


def pad_front(planes, axis_at):
    spread = [(0, 0)] * planes.ndim
    spread[axis_at] = (1, 0)
    return jnp.pad(planes, spread)

def pad_back(planes, axis_at):
    spread = [(0, 0)] * planes.ndim
    spread[axis_at] = (0, 1)
    return jnp.pad(planes, spread)

def reference(features, grad_out, weight, active):
    live_flags = active.astype(jnp.bfloat16)[..., None, None]
    stacked = jnp.stack([features * live_flags, grad_out * live_flags])
    bricks = stacked.reshape(2, COLS_X, COLS_Y, LEVELS, C, EDGE, EDGE, EDGE)
    top_cell = EDGE - 1
    west_rim = pad_front(bricks[:, :-1, :, :, :, top_cell], 1)
    east_rim = pad_back(bricks[:, 1:, :, :, :, 0], 1)
    south_rim = pad_front(bricks[:, :, :-1, :, :, :, top_cell], 2)
    north_rim = pad_back(bricks[:, :, 1:, :, :, :, 0], 2)
    below_rim = pad_front(bricks[:, :, :, :-1, :, :, :, top_cell], 3)
    above_rim = pad_back(bricks[:, :, :, 1:, :, :, :, 0], 3)
    brick_count = COLS_X * COLS_Y * LEVELS

    def by_brick(values):
        moved = jnp.moveaxis(values, 0, 3)
        return moved.reshape((brick_count,) + values.shape[:1] + values.shape[4:])
    brick_items = tuple((by_brick(values) for values in (bricks, west_rim, east_rim, south_rim, north_rim, below_rim, above_rim)))
    brick_items = brick_items + (active.reshape(brick_count),)
    weight_float = weight.astype(jnp.float32).reshape(C, 3, 3, 3, C)
    forward_kernel = jnp.transpose(weight_float, (0, 4, 1, 2, 3))
    backward_kernel = jnp.transpose(weight_float[:, ::-1, ::-1, ::-1, :], (4, 0, 1, 2, 3))
    numbers = ('NCDHW', 'OIDHW', 'NCDHW')

    def brick_step(grad_total, brick_item):
        one_brick, west_side, east_side, south_side, north_side, below_side, above_side, is_live = brick_item

        def compute(unused):
            padded = jnp.pad(one_brick.astype(jnp.float32), ((0, 0), (0, 0), (1, 1), (1, 1), (1, 1)))
            padded = padded.at[:, :, 0, 1:-1, 1:-1].set(west_side.astype(jnp.float32))
            padded = padded.at[:, :, -1, 1:-1, 1:-1].set(east_side.astype(jnp.float32))
            padded = padded.at[:, :, 1:-1, 0, 1:-1].set(south_side.astype(jnp.float32))
            padded = padded.at[:, :, 1:-1, -1, 1:-1].set(north_side.astype(jnp.float32))
            padded = padded.at[:, :, 1:-1, 1:-1, 0].set(below_side.astype(jnp.float32))
            padded = padded.at[:, :, 1:-1, 1:-1, -1].set(above_side.astype(jnp.float32))
            forward_res = lax.conv_general_dilated(padded[0:1], forward_kernel, (1, 1, 1), 'VALID', dimension_numbers=numbers, precision=lax.Precision.HIGHEST)
            backward_res = lax.conv_general_dilated(padded[1:2], backward_kernel, (1, 1, 1), 'VALID', dimension_numbers=numbers, precision=lax.Precision.HIGHEST)
            shifted = jnp.stack([padded[0, :, offset_x:offset_x + EDGE, offset_y:offset_y + EDGE, offset_z:offset_z + EDGE] for offset_x in range(3) for offset_y in range(3) for offset_z in range(3)])
            grad_part = jnp.einsum('cxyz,odxyz->cod', one_brick[1].astype(jnp.float32), shifted, precision=lax.Precision.HIGHEST)
            return (forward_res[0].reshape(C, VOX).astype(jnp.bfloat16), backward_res[0].reshape(C, VOX).astype(jnp.bfloat16), grad_part.reshape(C, 27 * C))

        def skipped(unused):
            return (jnp.zeros((C, VOX), jnp.bfloat16), jnp.zeros((C, VOX), jnp.bfloat16), jnp.zeros((C, 27 * C), jnp.float32))
        result_out, result_grad, grad_part = lax.cond(is_live > 0, compute, skipped, 0)
        return (grad_total + grad_part, (result_out, result_grad))
    start_total = jnp.zeros((C, 27 * C), jnp.float32)
    grad_total, (out_bricks, grad_bricks) = lax.scan(brick_step, start_total, brick_items)
    norm_scale = 1.0 / math.sqrt(brick_count * VOX)
    out = out_bricks.reshape(COLS_X, COLS_Y, LEVELS, C, VOX)
    grad_in = grad_bricks.reshape(COLS_X, COLS_Y, LEVELS, C, VOX)
    return (out, grad_in, (grad_total * norm_scale).reshape(KW))
```

```python
import functools
import math

import jax
import jax.numpy as jnp
from jax import lax
from jax.experimental import pallas as pl
from jax.experimental.pallas import tpu as pltpu
from jax.sharding import PartitionSpec as P

EDGE = 16
PLANE = EDGE * EDGE
MESH = pl.DeviceIdType.MESH
AXES = ("gx", "gy")


def lanes(shape):
    return lax.broadcasted_iota(jnp.int32, shape, 1)


def halo_kernel(counts, act_ref, f_ref, g_ref, out_ref, send, send_sem, recv_sem):
    levels, channels, _ = f_ref.shape
    here = [lax.axis_index(axis) for axis in AXES]
    faces = []
    for dim, axis in enumerate(AXES):
        for step in (-1, 1):
            exists = here[dim] > 0 if step < 0 else here[dim] < counts[dim] - 1
            faces.append((exists, {axis: here[dim] + step}))

    barrier = pltpu.get_barrier_semaphore()
    for exists, target in faces:

        @pl.when(exists)
        def _():
            pl.semaphore_signal(barrier, inc=1, device_id=target, device_id_type=MESH)

    rows = lanes((channels, PLANE)) // EDGE
    for which, ref in enumerate((f_ref, g_ref)):
        for level in range(levels):
            live = act_ref[0, level].astype(jnp.bfloat16)
            item = which * levels + level
            last = (EDGE - 1) * PLANE
            send[0, item] = ref[level, :, :PLANE] * live
            send[1, item] = ref[level, :, last : last + PLANE] * live
            south = jnp.zeros((channels, PLANE), jnp.float32)
            north = jnp.zeros((channels, PLANE), jnp.float32)
            for x in range(EDGE):
                plane = ref[level, :, x * PLANE : (x + 1) * PLANE].astype(jnp.float32)
                south = jnp.where(rows == x, pltpu.roll(plane, x * EDGE, 1), south)
                shift = (x * EDGE + EDGE) % PLANE
                north = jnp.where(rows == x, pltpu.roll(plane, shift, 1), north)
            send[2, item] = south.astype(jnp.bfloat16) * live
            send[3, item] = north.astype(jnp.bfloat16) * live

    peers = sum(exists.astype(jnp.int32) for exists, _target in faces)
    pl.semaphore_wait(barrier, peers)

    def copy_of(side):
        return pltpu.make_async_remote_copy(
            src_ref=send.at[side],
            dst_ref=out_ref.at[side ^ 1],
            send_sem=send_sem.at[side],
            recv_sem=recv_sem.at[side ^ 1],
            device_id=faces[side][1],
            device_id_type=MESH,
        )

    for side in range(4):

        @pl.when(faces[side][0])
        def _():
            copy_of(side).start()

        @pl.when(jnp.logical_not(faces[side][0]))
        def _():
            out_ref[side] = jnp.zeros(out_ref.shape[1:], jnp.bfloat16)

    for side in range(4):

        @pl.when(faces[side][0])
        def _():
            copy_of(side).wait_send()
            pltpu.make_async_remote_copy(
                src_ref=send.at[side],
                dst_ref=out_ref.at[side],
                send_sem=send_sem.at[side],
                recv_sem=recv_sem.at[side],
                device_id=faces[side][1],
                device_id_type=MESH,
            ).wait_recv()


def exchange(counts, act, f, g):
    levels, channels, _ = f.shape
    shape = (4, 2 * levels, channels, PLANE)
    return pl.pallas_call(
        functools.partial(halo_kernel, counts),
        out_shape=jax.ShapeDtypeStruct(shape, jnp.bfloat16),
        in_specs=[
            pl.BlockSpec(memory_space=pltpu.SMEM),
            pl.BlockSpec(memory_space=pltpu.VMEM),
            pl.BlockSpec(memory_space=pltpu.VMEM),
        ],
        out_specs=pl.BlockSpec(memory_space=pltpu.VMEM),
        scratch_shapes=[
            pltpu.VMEM(shape, jnp.bfloat16),
            pltpu.SemaphoreType.DMA((4,)),
            pltpu.SemaphoreType.DMA((4,)),
        ],
        compiler_params=pltpu.CompilerParams(
            collective_id=0, has_side_effects=True, vmem_limit_bytes=48 << 20
        ),
    )(act, f, g)


def brick_kernel(
    scale, act_ref, f_ref, g_ref, halo_ref, w_ref, out_ref, gin_ref, gw_ref,
    cube, other, own, taps, carry,
):
    levels, channels, _ = f_ref.shape
    depth = 9 * channels
    planes = EDGE + 2
    lane = lanes((channels, PLANE))
    y_at, z_at = lane // EDGE, lane % EDGE
    zero = jnp.zeros((channels, PLANE), jnp.bfloat16)

    gw_ref[...] = jnp.zeros_like(gw_ref)
    taps[...] = jnp.zeros_like(taps)
    for at in (0, 1, planes, planes + 1):
        own[at] = zero
    for which in range(2):
        for at in (0, planes - 1):
            other[which, at] = zero

    def roll(values, shift):
        return pltpu.roll(values, shift, 1)

    for level in range(levels):
        live = act_ref[0, level] > 0

        @pl.when(jnp.logical_not(live))
        def _():
            out_ref[level] = jnp.zeros_like(out_ref[level])
            gin_ref[level] = jnp.zeros_like(gin_ref[level])

        @pl.when(live)
        def _():
            assert levels <= 2
            near = level + 1 if level + 1 < levels else level - 1
            above = level + 1 < levels
            near_live = act_ref[0, near].astype(jnp.bfloat16) if levels > 1 else None
            for which, ref in enumerate((f_ref, g_ref)):
                item = which * levels + level
                cube[which, 0] = halo_ref[0, item]
                cube[which, planes - 1] = halo_ref[1, item]
                for x in range(EDGE):
                    part = slice(x * PLANE, (x + 1) * PLANE)
                    cube[which, x + 1] = ref[level, :, part]
                    if levels > 1:
                        other[which, x + 1] = ref[near, :, part] * near_live
                    else:
                        other[which, x + 1] = zero
                    if which == 1:
                        own[x + 2] = ref[level, :, part]
            carry[...] = jnp.zeros_like(carry)

            def build(at, slot):
                at = jnp.asarray(at, jnp.int32)
                inner = ((at >= 1) & (at <= EDGE)).astype(jnp.float32)
                base = (at - 1) * EDGE
                for which in range(2):
                    item = which * levels + level
                    here = cube[which, at].astype(jnp.float32)
                    side = other[which, at].astype(jnp.float32)
                    south = halo_ref[2, item].astype(jnp.float32) * inner
                    north = halo_ref[3, item].astype(jnp.float32) * inner
                    south = roll(south, (2 * PLANE - base) % PLANE)
                    north = roll(north, (2 * PLANE - EDGE - base) % PLANE)
                    for dy in (-1, 0, 1):
                        if dy < 0:
                            moved = jnp.where(y_at == 0, south, roll(here, EDGE))
                        elif dy > 0:
                            moved = jnp.where(y_at == EDGE - 1, north, roll(here, PLANE - EDGE))
                        else:
                            moved = here
                        edge = EDGE - 1 if above else 1 - EDGE
                        rim = roll(side, (edge - dy * EDGE) % PLANE)
                        if dy < 0:
                            rim = jnp.where(y_at == 0, 0.0, rim)
                        elif dy > 0:
                            rim = jnp.where(y_at == EDGE - 1, 0.0, rim)
                        low = jnp.where(z_at == 0, 0.0 if above else rim, roll(moved, 1))
                        high = jnp.where(
                            z_at == EDGE - 1, rim if above else 0.0, roll(moved, PLANE - 1)
                        )
                        for dz, value in ((-1, low), (0, moved), (1, high)):
                            tap = 3 * (dy + 1) + dz + 1
                            rows = pl.ds(tap * channels, channels)
                            taps[slot, which, rows, :] = value.astype(jnp.bfloat16)

            def multiply(at, slot):
                at = jnp.asarray(at, jnp.int32)
                target = pl.ds(pl.multiple_of(jnp.maximum(at - 2, 0) * PLANE, PLANE), PLANE)
                for which, ref in enumerate((out_ref, gin_ref)):
                    y = jnp.dot(
                        w_ref[which], taps[slot, which], preferred_element_type=jnp.float32
                    )
                    before, middle, after = (
                        y[i * channels : (i + 1) * channels] for i in range(3)
                    )
                    ref[level, :, target] = (after + carry[which, 0]).astype(jnp.bfloat16)
                    carry[which, 0] = middle + carry[which, 1]
                    carry[which, 1] = before
                grads = own[pl.ds(at, 3)].reshape(3 * channels, PLANE)
                gw_ref[...] += lax.dot_general(
                    grads,
                    taps[slot, 0, :depth, :],
                    (((1,), (1,)), ((), ())),
                    preferred_element_type=jnp.float32,
                )

            build(0, 0)

            def pair(i, unused):
                at = 2 * i
                build(at + 1, 1)
                multiply(at, 0)
                build(jnp.minimum(at + 2, planes - 1), 0)
                multiply(at + 1, 1)
                return unused

            lax.fori_loop(0, planes // 2, pair, 0)

    gw_ref[...] = gw_ref[...] * scale


def bricks(scale, act, f, g, halo, w):
    levels, channels, vox = f.shape
    depth = 9 * channels
    full = w.shape[-1]
    vmem = pl.BlockSpec(memory_space=pltpu.VMEM)
    like = jax.ShapeDtypeStruct(f.shape, jnp.bfloat16)
    return pl.pallas_call(
        functools.partial(brick_kernel, scale),
        out_shape=(like, like, jax.ShapeDtypeStruct((3 * channels, depth), jnp.float32)),
        in_specs=[pl.BlockSpec(memory_space=pltpu.SMEM)] + [vmem] * 4,
        out_specs=(vmem, vmem, vmem),
        scratch_shapes=[
            pltpu.VMEM((2, EDGE + 2, channels, PLANE), jnp.bfloat16),
            pltpu.VMEM((2, EDGE + 2, channels, PLANE), jnp.bfloat16),
            pltpu.VMEM((EDGE + 4, channels, PLANE), jnp.bfloat16),
            pltpu.VMEM((2, 2, full, PLANE), jnp.bfloat16),
            pltpu.VMEM((2, 2, channels, PLANE), jnp.float32),
        ],
        compiler_params=pltpu.CompilerParams(vmem_limit_bytes=56 << 20),
        cost_estimate=pl.CostEstimate(
            flops=levels * 6 * 27 * channels * channels * vox,
            bytes_accessed=8 * levels * channels * vox,
            transcendentals=0,
        ),
    )(act, f, g, halo, w)


def sum_kernel(stages, x_ref, out_ref, *scratch):
    count = len(stages)
    acc, recv = scratch[: count - 1], scratch[count - 1 : 2 * count - 1]
    send_sem, recv_sem = scratch[2 * count - 1 :]
    here = {axis: lax.axis_index(axis) for axis in AXES}
    partners = []
    for axis, step in stages:
        bit = here[axis] // step % 2
        partners.append((bit, {axis: here[axis] + step - 2 * step * bit}))
    barrier = pltpu.get_barrier_semaphore()
    for _bit, partner in partners:
        pl.semaphore_signal(barrier, inc=1, device_id=partner, device_id_type=MESH)
    pl.semaphore_wait(barrier, count)
    source = x_ref
    for stage, (bit, partner) in enumerate(partners):
        half = source.shape[0] // 2
        copy = pltpu.make_async_remote_copy(
            src_ref=source.at[pl.ds((1 - bit) * half, half)],
            dst_ref=recv[stage],
            send_sem=send_sem.at[stage],
            recv_sem=recv_sem.at[stage],
            device_id=partner,
            device_id_type=MESH,
        )
        copy.start()
        copy.wait()
        total = source[pl.ds(bit * half, half)] + recv[stage][...]
        if stage + 1 < count:
            acc[stage][...] = total
            source = acc[stage]
        else:
            out_ref[...] = total


def scatter_sum(stages, parts):
    vmem = pl.BlockSpec(memory_space=pltpu.VMEM)
    sizes = [parts.shape[0] >> (i + 1) for i in range(len(stages))]
    tail = parts.shape[1:]
    return pl.pallas_call(
        functools.partial(sum_kernel, stages),
        out_shape=jax.ShapeDtypeStruct((1,) + tail, jnp.float32),
        in_specs=[vmem],
        out_specs=vmem,
        scratch_shapes=[pltpu.VMEM((size,) + tail, jnp.float32) for size in sizes[:-1]]
        + [pltpu.VMEM((size,) + tail, jnp.float32) for size in sizes]
        + [pltpu.SemaphoreType.DMA((len(stages),))] * 2,
        compiler_params=pltpu.CompilerParams(
            collective_id=1, has_side_effects=True, vmem_limit_bytes=32 << 20
        ),
    )(parts)


def power_of_two(n):
    return n & (n - 1) == 0


def body(features, grad_out, weight, active):
    counts = [lax.axis_size(axis) for axis in AXES]
    levels, channels, vox = features.shape[2:]
    f, g, act = features[0, 0], grad_out[0, 0], active[0]
    halo = exchange(counts, act, f, g)
    cut = weight.reshape(channels, 3, 9, channels)
    ahead = cut.transpose(1, 0, 2, 3).reshape(3 * channels, 9 * channels)
    back = cut[:, ::-1, ::-1].transpose(1, 3, 2, 0).reshape(3 * channels, 9 * channels)
    w = jnp.stack([ahead, back])
    w = jnp.pad(w, ((0, 0), (0, 0), (0, -9 * channels % 128)))
    scale = 1.0 / math.sqrt(counts[0] * counts[1] * levels * vox)
    out, gin, gw = bricks(scale, act, f, g, halo, w)
    flat = gw.reshape(3, channels, 9 * channels)[::-1].transpose(1, 0, 2).reshape(-1)
    devices = counts[0] * counts[1]
    chunk = flat.shape[0] // devices
    if devices > 1 and all(map(power_of_two, counts)) and chunk % 8 == 0:
        bits = [count.bit_length() - 1 for count in counts]
        total = sum(bits)
        order = [bits[0] - 1 - i for i in range(bits[0])] + [total - 1 - i for i in range(bits[1])]
        parts = flat.reshape((2,) * total + (8, chunk // 8))
        parts = parts.transpose(order + [total, total + 1]).reshape(devices, 8, chunk // 8)
        stages = [(AXES[a], 1 << i) for a in range(2) for i in range(bits[a])]
        summed = scatter_sum(stages, parts).reshape(chunk)
    else:
        summed = lax.psum_scatter(flat, AXES, scatter_dimension=0, tiled=True)
    return out[None, None], gin[None, None], summed


def solution(mesh):
    placed = (P("gx", "gy", None, None, None), P("gx", "gy", None, None, None), P(), P("gx", "gy", None))
    return jax.shard_map(
        body,
        mesh=mesh,
        in_specs=placed,
        out_specs=(
            P("gx", "gy", None, None, None),
            P("gx", "gy", None, None, None),
            P(("gx", "gy")),
        ),
        check_vma=False,
    )
```

```python
import functools
import math

import jax
import jax.numpy as jnp
from jax import lax
from jax.experimental import pallas as pl
from jax.experimental.pallas import tpu as pltpu
from jax.sharding import PartitionSpec as P

EDGE = 16
PLANE = EDGE * EDGE
MESH = pl.DeviceIdType.MESH
AXES = ("gx", "gy")


def lanes(shape):
    return lax.broadcasted_iota(jnp.int32, shape, 1)


def side_faces(counts):
    here = [lax.axis_index(axis) for axis in AXES]
    faces = []
    for dim, axis in enumerate(AXES):
        for step in (-1, 1):
            exists = here[dim] > 0 if step < 0 else here[dim] < counts[dim] - 1
            faces.append((exists, {axis: here[dim] + step}))
    return faces


def fill_faces(act_ref, ref, send):
    levels, channels, _ = ref.shape
    rows = lanes((channels, PLANE)) // EDGE
    last = (EDGE - 1) * PLANE
    for level in range(levels):
        live = act_ref[0, level].astype(jnp.bfloat16)
        send[0, level] = ref[level, :, :PLANE] * live
        send[1, level] = ref[level, :, last : last + PLANE] * live
        south = jnp.zeros((channels, PLANE), jnp.float32)
        north = jnp.zeros((channels, PLANE), jnp.float32)
        for x in range(EDGE):
            plane = ref[level, :, x * PLANE : (x + 1) * PLANE].astype(jnp.float32)
            south = jnp.where(rows == x, pltpu.roll(plane, x * EDGE, 1), south)
            shift = (x * EDGE + EDGE) % PLANE
            north = jnp.where(rows == x, pltpu.roll(plane, shift, 1), north)
        send[2, level] = south.astype(jnp.bfloat16) * live
        send[3, level] = north.astype(jnp.bfloat16) * live


def face_copy(faces, send, recv, send_sem, recv_sem, side, slot):
    return pltpu.make_async_remote_copy(
        src_ref=send.at[side],
        dst_ref=recv.at[slot],
        send_sem=send_sem.at[side],
        recv_sem=recv_sem.at[slot],
        device_id=faces[side][1],
        device_id_type=MESH,
    )


def send_faces(faces, send, recv, send_sem, recv_sem):
    for side in range(4):

        @pl.when(faces[side][0])
        def _():
            face_copy(faces, send, recv, send_sem, recv_sem, side, side ^ 1).start()

        @pl.when(jnp.logical_not(faces[side][0]))
        def _():
            recv[side] = jnp.zeros(recv.shape[1:], jnp.bfloat16)


def await_faces(faces, send, recv, send_sem, recv_sem):
    for side in range(4):

        @pl.when(faces[side][0])
        def _():
            face_copy(faces, send, recv, send_sem, recv_sem, side, side ^ 1).wait_send()
            face_copy(faces, send, recv, send_sem, recv_sem, side, side).wait_recv()


def lay_cube(act_ref, ref, cube):
    levels, channels, _ = ref.shape
    zero = jnp.zeros((channels, PLANE), jnp.bfloat16)
    for level in range(levels):
        live = act_ref[0, level].astype(jnp.bfloat16)
        cube[level, 0] = zero
        cube[level, EDGE + 1] = zero
        for x in range(EDGE):
            cube[level, x + 1] = ref[level, :, x * PLANE : (x + 1) * PLANE] * live


def build_taps(level, levels, cube, halo, taps, at, slot):
    channels = cube.shape[2]
    lane = lanes((channels, PLANE))
    y_at, z_at = lane // EDGE, lane % EDGE
    at = jnp.asarray(at, jnp.int32)

    def roll(values, shift):
        return pltpu.roll(values, shift, 1)

    inner = ((at >= 1) & (at <= EDGE)).astype(jnp.float32)
    base = (at - 1) * EDGE
    west = (at == 0).astype(jnp.bfloat16)
    east = (at == EDGE + 1).astype(jnp.bfloat16)
    here = cube[level, at] + halo[0, level] * west + halo[1, level] * east
    here = here.astype(jnp.float32)
    south = halo[2, level].astype(jnp.float32) * inner
    north = halo[3, level].astype(jnp.float32) * inner
    south = roll(south, (2 * PLANE - base) % PLANE)
    north = roll(north, (2 * PLANE - EDGE - base) % PLANE)
    nears = [cube[k, at].astype(jnp.float32) if 0 <= k < levels else None
             for k in (level - 1, level + 1)]
    for dy in (-1, 0, 1):
        if dy < 0:
            moved = jnp.where(y_at == 0, south, roll(here, EDGE))
        elif dy > 0:
            moved = jnp.where(y_at == EDGE - 1, north, roll(here, PLANE - EDGE))
        else:
            moved = here
        rims = []
        for near, edge in zip(nears, (1 - EDGE, EDGE - 1)):
            if near is None:
                rims.append(0.0)
                continue
            rim = roll(near, (edge - dy * EDGE) % PLANE)
            if dy < 0:
                rim = jnp.where(y_at == 0, 0.0, rim)
            elif dy > 0:
                rim = jnp.where(y_at == EDGE - 1, 0.0, rim)
            rims.append(rim)
        low = jnp.where(z_at == 0, rims[0], roll(moved, 1))
        high = jnp.where(z_at == EDGE - 1, rims[1], roll(moved, PLANE - 1))
        for dz, value in ((-1, low), (0, moved), (1, high)):
            tap = 3 * (dy + 1) + dz + 1
            taps[slot, pl.ds(tap * channels, channels), :] = value.astype(jnp.bfloat16)


def add_plane(w, live, level, taps, carry, ref, at, slot):
    channels = carry.shape[1]
    at = jnp.asarray(at, jnp.int32)
    target = pl.ds(pl.multiple_of(jnp.maximum(at - 2, 0) * PLANE, PLANE), PLANE)
    y = jnp.dot(w[...], taps[slot], preferred_element_type=jnp.float32)
    before, middle, after = (y[i * channels : (i + 1) * channels] for i in range(3))
    ref[level, :, target] = ((after + carry[0]) * live).astype(jnp.bfloat16)
    carry[0] = middle + carry[1]
    carry[1] = before


def run_pairs(first, end, build, multiply):
    def pair(i, unused):
        at = 2 * i
        build(at + 1, 1)
        multiply(at, 0)
        build(jnp.minimum(at + 2, EDGE + 1), 0)
        multiply(at + 1, 1)
        return unused

    lax.fori_loop(first, end, pair, 0)


def ahead_kernel(
    counts, scale, act_ref, f_ref, g_ref, weight_ref, out_ref, gw_ref, w_back, halo_g,
    w, halo_f, send_f, send_g, cube, own, taps, carry, gw, f_sem, f_recv, g_sem, g_recv,
):
    levels, channels, _ = f_ref.shape
    depth = 9 * channels
    faces = side_faces(counts)
    barrier = pltpu.get_barrier_semaphore()
    for exists, target in faces:

        @pl.when(exists)
        def _():
            pl.semaphore_signal(barrier, inc=1, device_id=target, device_id_type=MESH)

    fill_faces(act_ref, f_ref, send_f)
    pl.semaphore_wait(barrier, sum(exists.astype(jnp.int32) for exists, _target in faces))
    send_faces(faces, send_f, halo_f, f_sem, f_recv)
    fill_faces(act_ref, g_ref, send_g)
    send_faces(faces, send_g, halo_g, g_sem, g_recv)

    wide = weight_ref[...].astype(jnp.float32)
    w[...] = jnp.zeros_like(w)
    w_back[...] = jnp.zeros_like(w_back)
    for dx in range(3):
        rows = slice(dx * channels, (dx + 1) * channels)
        w[rows, :depth] = wide[:, dx * depth : (dx + 1) * depth].astype(jnp.bfloat16)
        blocks = []
        for tap in range(9):
            start = ((2 - dx) * 9 + 8 - tap) * channels
            blocks.append(wide[:, start : start + channels].T)
        w_back[rows, :depth] = jnp.concatenate(blocks, axis=1).astype(jnp.bfloat16)

    lay_cube(act_ref, f_ref, cube)
    taps[...] = jnp.zeros_like(taps)
    gw[...] = jnp.zeros_like(gw)
    zero = jnp.zeros((channels, PLANE), jnp.bfloat16)
    for at in (0, 1, EDGE + 2, EDGE + 3):
        own[at] = zero
    await_faces(faces, send_f, halo_f, f_sem, f_recv)

    for level in range(levels):
        live = act_ref[0, level]
        for x in range(EDGE):
            plane = g_ref[level, :, x * PLANE : (x + 1) * PLANE]
            own[x + 2] = plane * live.astype(jnp.bfloat16)
        carry[...] = jnp.zeros_like(carry)

        def build(at, slot):
            build_taps(level, levels, cube, halo_f, taps, at, slot)

        def multiply(at, slot):
            add_plane(w, live.astype(jnp.float32), level, taps, carry, out_ref, at, slot)
            grads = own[pl.ds(at, 3)].reshape(3 * channels, PLANE)
            gw[...] += lax.dot_general(
                grads,
                taps[slot, :depth, :],
                (((1,), (1,)), ((), ())),
                preferred_element_type=jnp.float32,
            )

        build(0, 0)
        run_pairs(0, EDGE // 2 + 1, build, multiply)

    for dx in range(3):
        gw_ref[dx] = gw[(2 - dx) * channels : (3 - dx) * channels, :] * scale
    await_faces(faces, send_g, halo_g, g_sem, g_recv)


def ahead(counts, scale, act, f, g, weight):
    levels, channels, vox = f.shape
    depth = 9 * channels
    full = depth + -depth % 128
    vmem = pl.BlockSpec(memory_space=pltpu.VMEM)
    halo = (4, levels, channels, PLANE)
    return pl.pallas_call(
        functools.partial(ahead_kernel, counts, scale),
        out_shape=(
            jax.ShapeDtypeStruct(f.shape, jnp.bfloat16),
            jax.ShapeDtypeStruct((3, channels, depth), jnp.float32),
            jax.ShapeDtypeStruct((3 * channels, full), jnp.bfloat16),
            jax.ShapeDtypeStruct(halo, jnp.bfloat16),
        ),
        in_specs=[pl.BlockSpec(memory_space=pltpu.SMEM)] + [vmem] * 3,
        out_specs=(vmem,) * 4,
        scratch_shapes=[
            pltpu.VMEM((3 * channels, full), jnp.bfloat16),
            pltpu.VMEM(halo, jnp.bfloat16),
            pltpu.VMEM(halo, jnp.bfloat16),
            pltpu.VMEM(halo, jnp.bfloat16),
            pltpu.VMEM((levels, EDGE + 2, channels, PLANE), jnp.bfloat16),
            pltpu.VMEM((EDGE + 4, channels, PLANE), jnp.bfloat16),
            pltpu.VMEM((2, full, PLANE), jnp.bfloat16),
            pltpu.VMEM((2, channels, PLANE), jnp.float32),
            pltpu.VMEM((3 * channels, depth), jnp.float32),
        ]
        + [pltpu.SemaphoreType.DMA((4,))] * 4,
        compiler_params=pltpu.CompilerParams(
            collective_id=0, has_side_effects=True, vmem_limit_bytes=48 << 20
        ),
        cost_estimate=pl.CostEstimate(
            flops=levels * 4 * 27 * channels * channels * vox,
            bytes_accessed=8 * levels * channels * vox,
            transcendentals=0,
        ),
    )(act, f, g, weight)


def back_kernel(stages, act_ref, g_ref, halo_ref, w_ref, x_ref, gin_ref, sum_ref, *scratch):
    count = len(stages)
    acc, recv = scratch[: max(count - 1, 0)], scratch[max(count - 1, 0) : -5]
    cube, taps, carry, send_sem, recv_sem = scratch[-5:]
    levels, channels, _ = g_ref.shape
    here = {axis: lax.axis_index(axis) for axis in AXES}
    partners = []
    for axis, step in stages:
        bit = here[axis] // step % 2
        partners.append((bit, {axis: here[axis] + step - 2 * step * bit}))
    if count:
        barrier = pltpu.get_barrier_semaphore()
        for _bit, partner in partners:
            pl.semaphore_signal(barrier, inc=1, device_id=partner, device_id_type=MESH)
    sources = (x_ref,) + tuple(acc)

    def copy_of(stage):
        bit, partner = partners[stage]
        half = sources[stage].shape[0] // 2
        return pltpu.make_async_remote_copy(
            src_ref=sources[stage].at[pl.ds((1 - bit) * half, half)],
            dst_ref=recv[stage],
            send_sem=send_sem.at[stage],
            recv_sem=recv_sem.at[stage],
            device_id=partner,
            device_id_type=MESH,
        )

    def finish(stage):
        copy_of(stage).wait()
        half = sources[stage].shape[0] // 2
        bit = partners[stage][0]
        total = sources[stage][pl.ds(bit * half, half)] + recv[stage][...]
        if stage + 1 < count:
            acc[stage][...] = total
            copy_of(stage + 1).start()
        else:
            sum_ref[...] = total

    if count:
        pl.semaphore_wait(barrier, count)
        copy_of(0).start()
    else:
        sum_ref[...] = x_ref[...]

    lay_cube(act_ref, g_ref, cube)
    taps[...] = jnp.zeros_like(taps)
    pairs = EDGE // 2 + 1
    stops = [-(-levels * pairs * (i + 1) // (count + 1)) for i in range(count)]
    for level in range(levels):
        live = act_ref[0, level].astype(jnp.float32)
        carry[...] = jnp.zeros_like(carry)

        def build(at, slot):
            build_taps(level, levels, cube, halo_ref, taps, at, slot)

        def multiply(at, slot):
            add_plane(w_ref, live, level, taps, carry, gin_ref, at, slot)

        build(0, 0)
        at = 0
        for stage, stop in enumerate(stops):
            stop = stop - level * pairs
            if 0 < stop <= pairs:
                run_pairs(at, stop, build, multiply)
                at = stop
                finish(stage)
        if at < pairs:
            run_pairs(at, pairs, build, multiply)


def behind(stages, act, g, halo, w, parts):
    levels, channels, vox = g.shape
    vmem = pl.BlockSpec(memory_space=pltpu.VMEM)
    sizes = [parts.shape[0] >> (i + 1) for i in range(len(stages))]
    tail = parts.shape[1:]
    count = len(stages)
    return pl.pallas_call(
        functools.partial(back_kernel, stages),
        out_shape=(
            jax.ShapeDtypeStruct(g.shape, jnp.bfloat16),
            jax.ShapeDtypeStruct((parts.shape[0] >> count,) + tail, jnp.float32),
        ),
        in_specs=[pl.BlockSpec(memory_space=pltpu.SMEM)] + [vmem] * 4,
        out_specs=(vmem, vmem),
        scratch_shapes=[pltpu.VMEM((size,) + tail, jnp.float32) for size in sizes[:-1]]
        + [pltpu.VMEM((size,) + tail, jnp.float32) for size in sizes]
        + [
            pltpu.VMEM((levels, EDGE + 2, channels, PLANE), jnp.bfloat16),
            pltpu.VMEM((2, w.shape[1], PLANE), jnp.bfloat16),
            pltpu.VMEM((2, channels, PLANE), jnp.float32),
        ]
        + [pltpu.SemaphoreType.DMA((max(count, 1),))] * 2,
        compiler_params=pltpu.CompilerParams(
            collective_id=1 if count else None, has_side_effects=True, vmem_limit_bytes=48 << 20
        ),
        cost_estimate=pl.CostEstimate(
            flops=levels * 2 * 27 * channels * channels * vox,
            bytes_accessed=8 * levels * channels * vox,
            transcendentals=0,
        ),
    )(act, g, halo, w, parts)


def power_of_two(n):
    return n & (n - 1) == 0


def body(features, grad_out, weight, active):
    counts = [lax.axis_size(axis) for axis in AXES]
    levels, channels, vox = features.shape[2:]
    f, g, act = features[0, 0], grad_out[0, 0], active[0]
    scale = 1.0 / math.sqrt(counts[0] * counts[1] * levels * vox)
    out, gw, w_back, halo = ahead(counts, scale, act, f, g, weight)
    flat = gw.transpose(1, 0, 2).reshape(-1)
    devices = counts[0] * counts[1]
    chunk = flat.shape[0] // devices
    if devices > 1 and all(map(power_of_two, counts)) and chunk % 8 == 0:
        bits = [count.bit_length() - 1 for count in counts]
        total = sum(bits)
        order = [bits[0] - 1 - i for i in range(bits[0])] + [total - 1 - i for i in range(bits[1])]
        parts = flat.reshape((2,) * total + (8, chunk // 8))
        parts = parts.transpose(order + [total, total + 1]).reshape(devices, 8, chunk // 8)
        stages = [(AXES[a], 1 << i) for a in range(2) for i in range(bits[a])]
        gin, summed = behind(stages, act, g, halo, w_back, parts)
        summed = summed.reshape(chunk)
    else:
        gin, _ = behind([], act, g, halo, w_back, jnp.zeros((1, 8, 128), jnp.float32))
        summed = lax.psum_scatter(flat, AXES, scatter_dimension=0, tiled=True)
    return out[None, None], gin[None, None], summed


def solution(mesh):
    placed = (P("gx", "gy", None, None, None), P("gx", "gy", None, None, None), P(), P("gx", "gy", None))
    return jax.shard_map(
        body,
        mesh=mesh,
        in_specs=placed,
        out_specs=(
            P("gx", "gy", None, None, None),
            P("gx", "gy", None, None, None),
            P(("gx", "gy")),
        ),
        check_vma=False,
    )
```

```python
import functools
import math

import jax
import jax.numpy as jnp
from jax import lax
from jax.experimental import pallas as pl
from jax.experimental.pallas import tpu as pltpu
from jax.sharding import PartitionSpec as P

EDGE = 16
PLANE = EDGE * EDGE
MESH = pl.DeviceIdType.MESH
AXES = ("gx", "gy")


def lanes(shape):
    return lax.broadcasted_iota(jnp.int32, shape, 1)


def side_faces(counts):
    here = [lax.axis_index(axis) for axis in AXES]
    faces = []
    for dim, axis in enumerate(AXES):
        for step in (-1, 1):
            exists = here[dim] > 0 if step < 0 else here[dim] < counts[dim] - 1
            faces.append((exists, {axis: here[dim] + step}))
    return faces


def fill_faces(act_ref, ref, send):
    levels, channels, _ = ref.shape
    rows = lanes((channels, PLANE)) // EDGE
    last = (EDGE - 1) * PLANE
    for level in range(levels):
        live = act_ref[0, level].astype(jnp.bfloat16)
        send[0, level] = ref[level, :, :PLANE] * live
        send[1, level] = ref[level, :, last : last + PLANE] * live
        south = jnp.zeros((channels, PLANE), jnp.float32)
        north = jnp.zeros((channels, PLANE), jnp.float32)
        for x in range(EDGE):
            plane = ref[level, :, x * PLANE : (x + 1) * PLANE].astype(jnp.float32)
            south = jnp.where(rows == x, pltpu.roll(plane, x * EDGE, 1), south)
            shift = (x * EDGE + EDGE) % PLANE
            north = jnp.where(rows == x, pltpu.roll(plane, shift, 1), north)
        send[2, level] = south.astype(jnp.bfloat16) * live
        send[3, level] = north.astype(jnp.bfloat16) * live


def face_copy(faces, send, recv, send_sem, recv_sem, side, slot):
    return pltpu.make_async_remote_copy(
        src_ref=send.at[side],
        dst_ref=recv.at[slot],
        send_sem=send_sem.at[side],
        recv_sem=recv_sem.at[slot],
        device_id=faces[side][1],
        device_id_type=MESH,
    )


def send_faces(faces, send, recv, send_sem, recv_sem):
    for side in range(4):

        @pl.when(faces[side][0])
        def _():
            face_copy(faces, send, recv, send_sem, recv_sem, side, side ^ 1).start()

        @pl.when(jnp.logical_not(faces[side][0]))
        def _():
            recv[side] = jnp.zeros(recv.shape[1:], jnp.bfloat16)


def await_faces(faces, send, recv, send_sem, recv_sem):
    for side in range(4):

        @pl.when(faces[side][0])
        def _():
            face_copy(faces, send, recv, send_sem, recv_sem, side, side ^ 1).wait_send()
            face_copy(faces, send, recv, send_sem, recv_sem, side, side).wait_recv()


def lay_cube(act_ref, ref, cube):
    levels, channels, _ = ref.shape
    zero = jnp.zeros((channels, PLANE), jnp.bfloat16)
    for level in range(levels):
        live = act_ref[0, level].astype(jnp.bfloat16)
        cube[level, 0] = zero
        cube[level, EDGE + 1] = zero
        for x in range(EDGE):
            cube[level, x + 1] = ref[level, :, x * PLANE : (x + 1) * PLANE] * live


def shift_nine(here, south, north, nears, taps, slot):
    channels = here.shape[0]
    lane = lanes((channels, PLANE))
    y_at, z_at = lane // EDGE, lane % EDGE

    def roll(values, shift):
        return pltpu.roll(values, shift, 1)

    for dy in (-1, 0, 1):
        if dy < 0:
            moved = jnp.where(y_at == 0, south, roll(here, EDGE))
        elif dy > 0:
            moved = jnp.where(y_at == EDGE - 1, north, roll(here, PLANE - EDGE))
        else:
            moved = here
        rims = []
        for near, edge in zip(nears, (1 - EDGE, EDGE - 1)):
            if near is None:
                rims.append(0.0)
                continue
            rim = roll(near, (edge - dy * EDGE) % PLANE)
            if dy < 0:
                rim = jnp.where(y_at == 0, 0.0, rim)
            elif dy > 0:
                rim = jnp.where(y_at == EDGE - 1, 0.0, rim)
            rims.append(rim)
        low = jnp.where(z_at == 0, rims[0], roll(moved, 1))
        high = jnp.where(z_at == EDGE - 1, rims[1], roll(moved, PLANE - 1))
        for dz, value in ((-1, low), (0, moved), (1, high)):
            tap = 3 * (dy + 1) + dz + 1
            taps[slot, pl.ds(tap * channels, channels), :] = value.astype(jnp.bfloat16)


def near_planes(cube, level, at):
    levels = cube.shape[0]
    return [
        cube[k, at].astype(jnp.float32) if 0 <= k < levels else None for k in (level - 1, level + 1)
    ]


def build_taps(level, cube, halo, taps, at, slot):
    at = jnp.asarray(at, jnp.int32)
    inner = ((at >= 1) & (at <= EDGE)).astype(jnp.float32)
    base = (at - 1) * EDGE
    west = (at == 0).astype(jnp.bfloat16)
    east = (at == EDGE + 1).astype(jnp.bfloat16)
    here = cube[level, at] + halo[0, level] * west + halo[1, level] * east
    south = halo[2, level].astype(jnp.float32) * inner
    north = halo[3, level].astype(jnp.float32) * inner
    south = pltpu.roll(south, (2 * PLANE - base) % PLANE, 1)
    north = pltpu.roll(north, (2 * PLANE - EDGE - base) % PLANE, 1)
    shift_nine(here.astype(jnp.float32), south, north, near_planes(cube, level, at), taps, slot)


def add_plane(w, live, level, taps, carry, ref, at, slot):
    channels = carry.shape[1]
    at = jnp.asarray(at, jnp.int32)
    target = pl.ds(pl.multiple_of(jnp.maximum(at - 2, 0) * PLANE, PLANE), PLANE)
    y = jnp.dot(w, taps[slot], preferred_element_type=jnp.float32)
    before, middle, after = (y[i * channels : (i + 1) * channels] for i in range(3))
    ref[level, :, target] = ((after + carry[0]) * live).astype(jnp.bfloat16)
    carry[0] = middle + carry[1]
    carry[1] = before


def run_pairs(first, end, build, multiply, base=0):
    def pair(i, unused):
        at = base + 2 * i
        build(at + 1, 1)
        multiply(at, 0)
        build(jnp.minimum(at + 2, EDGE + 1), 0)
        multiply(at + 1, 1)
        return unused

    lax.fori_loop(first, end, pair, 0)


def ahead_kernel(
    counts, scale, act_ref, f_ref, g_ref, gw_ref, halo_f, halo_g,
    send_f, send_g, cube, own, taps, gw, edges, f_sem, f_recv, g_sem, g_recv,
):
    levels, channels, _ = f_ref.shape
    depth = 9 * channels
    faces = side_faces(counts)
    barrier = pltpu.get_barrier_semaphore()
    for exists, target in faces:

        @pl.when(exists)
        def _():
            pl.semaphore_signal(barrier, inc=1, device_id=target, device_id_type=MESH)

    fill_faces(act_ref, f_ref, send_f)
    pl.semaphore_wait(barrier, sum(exists.astype(jnp.int32) for exists, _target in faces))
    send_faces(faces, send_f, halo_f, f_sem, f_recv)
    fill_faces(act_ref, g_ref, send_g)
    send_faces(faces, send_g, halo_g, g_sem, g_recv)

    lay_cube(act_ref, f_ref, cube)
    gw[...] = jnp.zeros_like(gw)
    zero = jnp.zeros((channels, PLANE), jnp.bfloat16)
    for level in range(levels):
        live = act_ref[0, level].astype(jnp.bfloat16)
        for at in (0, 1, EDGE + 2, EDGE + 3):
            own[level, at] = zero
        for x in range(EDGE):
            own[level, x + 2] = g_ref[level, :, x * PLANE : (x + 1) * PLANE] * live

    def product(left, slot):
        return lax.dot_general(
            left, taps[slot], (((1,), (1,)), ((), ())), preferred_element_type=jnp.float32
        )

    for level in range(levels):

        def build(at, slot):
            here = cube[level, at].astype(jnp.float32)
            shift_nine(here, 0.0, 0.0, near_planes(cube, level, at), taps, slot)

        def multiply(at, slot):
            gw[...] += product(own[level, pl.ds(at, 3)].reshape(3 * channels, PLANE), slot)

        build(1, 0)
        run_pairs(0, EDGE // 2, build, multiply, 1)

    await_faces(faces, send_f, halo_f, f_sem, f_recv)
    for level in range(levels):
        for slot, at in enumerate((0, EDGE + 1)):
            here = halo_f[slot, level].astype(jnp.float32)
            shift_nine(here, 0.0, 0.0, (None, None), taps, slot)
            gw[...] += product(own[level, pl.ds(at, 3)].reshape(3 * channels, PLANE), slot)
        for slot in range(2):
            here = halo_f[2 + slot, level].astype(jnp.float32)
            shift_nine(here, 0.0, 0.0, (None, None), taps, slot)
            term = product(send_g[2 + slot, level], slot)
            edges[slot] = edges[slot] + term if level else term

    third = depth // 3
    for dx in range(3):
        part = slice(dx * third, (dx + 1) * third)
        rows = gw[(2 - dx) * channels : (3 - dx) * channels, :]
        south = rows[:, :third] + edges[0][:, part]
        north = rows[:, 2 * third :] + edges[1][:, part]
        joined = jnp.concatenate([south, rows[:, third : 2 * third], north], axis=1)
        gw_ref[dx] = joined * scale
    await_faces(faces, send_g, halo_g, g_sem, g_recv)


def ahead(counts, scale, act, f, g):
    levels, channels, vox = f.shape
    depth = 9 * channels
    vmem = pl.BlockSpec(memory_space=pltpu.VMEM)
    halo = (4, levels, channels, PLANE)
    return pl.pallas_call(
        functools.partial(ahead_kernel, counts, scale),
        out_shape=(
            jax.ShapeDtypeStruct((3, channels, depth), jnp.float32),
            jax.ShapeDtypeStruct(halo, jnp.bfloat16),
            jax.ShapeDtypeStruct(halo, jnp.bfloat16),
        ),
        in_specs=[pl.BlockSpec(memory_space=pltpu.SMEM)] + [vmem] * 2,
        out_specs=(vmem,) * 3,
        scratch_shapes=[
            pltpu.VMEM(halo, jnp.bfloat16),
            pltpu.VMEM(halo, jnp.bfloat16),
            pltpu.VMEM((levels, EDGE + 2, channels, PLANE), jnp.bfloat16),
            pltpu.VMEM((levels, EDGE + 4, channels, PLANE), jnp.bfloat16),
            pltpu.VMEM((2, depth, PLANE), jnp.bfloat16),
            pltpu.VMEM((3 * channels, depth), jnp.float32),
            pltpu.VMEM((2, channels, depth), jnp.float32),
        ]
        + [pltpu.SemaphoreType.DMA((4,))] * 4,
        compiler_params=pltpu.CompilerParams(
            collective_id=0, has_side_effects=True, vmem_limit_bytes=48 << 20
        ),
        cost_estimate=pl.CostEstimate(
            flops=levels * 2 * 27 * channels * channels * vox,
            bytes_accessed=8 * levels * channels * vox,
            transcendentals=0,
        ),
    )(act, f, g)


def lay_weights(weight_ref, w):
    channels = weight_ref.shape[0]
    depth = 9 * channels
    wide = weight_ref[...].astype(jnp.float32)
    w[...] = jnp.zeros_like(w)
    for dx in range(3):
        rows = slice(dx * channels, (dx + 1) * channels)
        w[0, rows, :depth] = wide[:, dx * depth : (dx + 1) * depth].astype(jnp.bfloat16)
        blocks = []
        for tap in range(9):
            start = ((2 - dx) * 9 + 8 - tap) * channels
            blocks.append(wide[:, start : start + channels].T)
        w[1, rows, :depth] = jnp.concatenate(blocks, axis=1).astype(jnp.bfloat16)


def back_kernel(
    stages, act_ref, f_ref, g_ref, halo_f, halo_g, weight_ref, x_ref, out_ref, gin_ref, sum_ref,
    *scratch,
):
    count = len(stages)
    acc, recv = scratch[: max(count - 1, 0)], scratch[max(count - 1, 0) : -6]
    cube, taps, carry, w, send_sem, recv_sem = scratch[-6:]
    levels, channels, _ = g_ref.shape
    here = {axis: lax.axis_index(axis) for axis in AXES}
    partners = []
    for axis, step in stages:
        bit = here[axis] // step % 2
        partners.append((bit, {axis: here[axis] + step - 2 * step * bit}))
    if count:
        barrier = pltpu.get_barrier_semaphore()
        for _bit, partner in partners:
            pl.semaphore_signal(barrier, inc=1, device_id=partner, device_id_type=MESH)
    sources = (x_ref,) + tuple(acc)

    def copy_of(stage):
        bit, partner = partners[stage]
        half = sources[stage].shape[0] // 2
        return pltpu.make_async_remote_copy(
            src_ref=sources[stage].at[pl.ds((1 - bit) * half, half)],
            dst_ref=recv[stage],
            send_sem=send_sem.at[stage],
            recv_sem=recv_sem.at[stage],
            device_id=partner,
            device_id_type=MESH,
        )

    def finish(stage):
        copy_of(stage).wait()
        half = sources[stage].shape[0] // 2
        bit = partners[stage][0]
        total = sources[stage][pl.ds(bit * half, half)] + recv[stage][...]
        if stage + 1 < count:
            acc[stage][...] = total
            copy_of(stage + 1).start()
        else:
            sum_ref[...] = total

    if count:
        pl.semaphore_wait(barrier, count)
        copy_of(0).start()
    else:
        sum_ref[...] = x_ref[...]

    lay_weights(weight_ref, w)
    taps[...] = jnp.zeros_like(taps)
    lay_cube(act_ref, f_ref, cube.at[0])
    lay_cube(act_ref, g_ref, cube.at[1])
    pairs = EDGE // 2 + 1
    lengths = [1.2 + 5 * 0.5 ** (i - 1) if i else 2.0 for i in range(count)]
    stops = [round(levels * pairs * sum(lengths[: i + 1]) / sum(lengths)) for i in range(count)]
    for level in range(levels):
        live = act_ref[0, level].astype(jnp.float32)
        carry[...] = jnp.zeros_like(carry)
        work = ((halo_f, out_ref), (halo_g, gin_ref))

        def build(at, slot):
            for k, (halo, _ref) in enumerate(work):
                build_taps(level, cube.at[k], halo, taps.at[k], at, slot)

        def multiply(at, slot):
            for k, (_halo, ref) in enumerate(work):
                add_plane(w[k], live, level, taps.at[k], carry.at[k], ref, at, slot)

        build(0, 0)
        at = 0
        for stage, stop in enumerate(stops):
            stop = stop - level * pairs
            if 0 < stop <= pairs:
                run_pairs(at, stop, build, multiply)
                at = stop
                finish(stage)
        if at < pairs:
            run_pairs(at, pairs, build, multiply)


def behind(stages, act, f, g, halo_f, halo_g, weight, parts):
    levels, channels, vox = g.shape
    full = 9 * channels + -9 * channels % 128
    vmem = pl.BlockSpec(memory_space=pltpu.VMEM)
    sizes = [parts.shape[0] >> (i + 1) for i in range(len(stages))]
    tail = parts.shape[1:]
    count = len(stages)
    return pl.pallas_call(
        functools.partial(back_kernel, stages),
        out_shape=(
            jax.ShapeDtypeStruct(f.shape, jnp.bfloat16),
            jax.ShapeDtypeStruct(g.shape, jnp.bfloat16),
            jax.ShapeDtypeStruct((parts.shape[0] >> count,) + tail, jnp.float32),
        ),
        in_specs=[pl.BlockSpec(memory_space=pltpu.SMEM)] + [vmem] * 6,
        out_specs=(vmem, vmem, vmem),
        scratch_shapes=[pltpu.VMEM((size,) + tail, jnp.float32) for size in sizes[:-1]]
        + [pltpu.VMEM((size,) + tail, jnp.float32) for size in sizes]
        + [
            pltpu.VMEM((2, levels, EDGE + 2, channels, PLANE), jnp.bfloat16),
            pltpu.VMEM((2, 2, full, PLANE), jnp.bfloat16),
            pltpu.VMEM((2, 2, channels, PLANE), jnp.float32),
            pltpu.VMEM((2, 3 * channels, full), jnp.bfloat16),
        ]
        + [pltpu.SemaphoreType.DMA((max(count, 1),))] * 2,
        compiler_params=pltpu.CompilerParams(
            collective_id=1 if count else None, has_side_effects=True, vmem_limit_bytes=48 << 20
        ),
        cost_estimate=pl.CostEstimate(
            flops=levels * 4 * 27 * channels * channels * vox,
            bytes_accessed=16 * levels * channels * vox,
            transcendentals=0,
        ),
    )(act, f, g, halo_f, halo_g, weight, parts)


def power_of_two(n):
    return n & (n - 1) == 0


def body(features, grad_out, weight, active):
    counts = [lax.axis_size(axis) for axis in AXES]
    levels, channels, vox = features.shape[2:]
    f, g, act = features[0, 0], grad_out[0, 0], active[0]
    scale = 1.0 / math.sqrt(counts[0] * counts[1] * levels * vox)
    gw, halo_f, halo_g = ahead(counts, scale, act, f, g)
    operands = (act, f, g, halo_f, halo_g, weight)
    flat = gw.transpose(1, 0, 2).reshape(-1)
    devices = counts[0] * counts[1]
    chunk = flat.shape[0] // devices
    if devices > 1 and all(map(power_of_two, counts)) and chunk % 8 == 0:
        bits = [count.bit_length() - 1 for count in counts]
        total = sum(bits)
        order = [bits[0] - 1 - i for i in range(bits[0])] + [total - 1 - i for i in range(bits[1])]
        parts = flat.reshape((2,) * total + (8, chunk // 8))
        parts = parts.transpose(order + [total, total + 1]).reshape(devices, 8, chunk // 8)
        stages = [(AXES[a], 1 << i) for a in range(2) for i in range(bits[a])]
        out, gin, summed = behind(stages, *operands, parts)
        summed = summed.reshape(chunk)
    else:
        out, gin, _ = behind([], *operands, jnp.zeros((1, 8, 128), jnp.float32))
        summed = lax.psum_scatter(flat, AXES, scatter_dimension=0, tiled=True)
    return out[None, None], gin[None, None], summed


def solution(mesh):
    placed = (P("gx", "gy", None, None, None), P("gx", "gy", None, None, None), P(), P("gx", "gy", None))
    return jax.shard_map(
        body,
        mesh=mesh,
        in_specs=placed,
        out_specs=(
            P("gx", "gy", None, None, None),
            P("gx", "gy", None, None, None),
            P(("gx", "gy")),
        ),
        check_vma=False,
    )
```

```python
import functools
import math

import jax
import jax.numpy as jnp
from jax import lax
from jax.experimental import pallas as pl
from jax.experimental.pallas import tpu as pltpu
from jax.sharding import PartitionSpec as P

EDGE = 16
PLANE = EDGE * EDGE
MESH = pl.DeviceIdType.MESH
AXES = ("gx", "gy")


def lanes(shape):
    return lax.broadcasted_iota(jnp.int32, shape, 1)


def side_faces(counts):
    here = [lax.axis_index(axis) for axis in AXES]
    faces = []
    for dim, axis in enumerate(AXES):
        for step in (-1, 1):
            exists = here[dim] > 0 if step < 0 else here[dim] < counts[dim] - 1
            faces.append((exists, {axis: here[dim] + step}))
    return faces


def fill_faces(act_ref, ref, send):
    levels, channels, _ = ref.shape
    rows = lanes((channels, PLANE)) // EDGE
    last = (EDGE - 1) * PLANE
    for level in range(levels):
        live = act_ref[0, level].astype(jnp.bfloat16)
        send[0, level] = ref[level, :, :PLANE] * live
        send[1, level] = ref[level, :, last : last + PLANE] * live
        south = jnp.zeros((channels, PLANE), jnp.float32)
        north = jnp.zeros((channels, PLANE), jnp.float32)
        for x in range(EDGE):
            plane = ref[level, :, x * PLANE : (x + 1) * PLANE].astype(jnp.float32)
            south = jnp.where(rows == x, pltpu.roll(plane, x * EDGE, 1), south)
            shift = (x * EDGE + EDGE) % PLANE
            north = jnp.where(rows == x, pltpu.roll(plane, shift, 1), north)
        send[2, level] = south.astype(jnp.bfloat16) * live
        send[3, level] = north.astype(jnp.bfloat16) * live


def face_copy(faces, send, recv, send_sem, recv_sem, side, slot):
    return pltpu.make_async_remote_copy(
        src_ref=send.at[side],
        dst_ref=recv.at[slot],
        send_sem=send_sem.at[side],
        recv_sem=recv_sem.at[slot],
        device_id=faces[side][1],
        device_id_type=MESH,
    )


def send_faces(faces, send, recv, send_sem, recv_sem):
    for side in range(4):

        @pl.when(faces[side][0])
        def _():
            face_copy(faces, send, recv, send_sem, recv_sem, side, side ^ 1).start()

        @pl.when(jnp.logical_not(faces[side][0]))
        def _():
            recv[side] = jnp.zeros(recv.shape[1:], jnp.bfloat16)


def await_faces(faces, send, recv, send_sem, recv_sem):
    for side in range(4):

        @pl.when(faces[side][0])
        def _():
            face_copy(faces, send, recv, send_sem, recv_sem, side, side ^ 1).wait_send()
            face_copy(faces, send, recv, send_sem, recv_sem, side, side).wait_recv()


def lay_cube(act_ref, ref, cube):
    levels, channels, _ = ref.shape
    zero = jnp.zeros((channels, PLANE), jnp.bfloat16)
    for level in range(levels):
        live = act_ref[0, level].astype(jnp.bfloat16)
        cube[level, 0] = zero
        cube[level, EDGE + 1] = zero
        for x in range(EDGE):
            cube[level, x + 1] = ref[level, :, x * PLANE : (x + 1) * PLANE] * live


def shift_nine(here, south, north, nears, taps, slot):
    channels = here.shape[0]
    lane = lanes((channels, PLANE))
    y_at, z_at = lane // EDGE, lane % EDGE

    def roll(values, shift):
        return pltpu.roll(values, shift, 1)

    for dy in (-1, 0, 1):
        if dy < 0:
            moved = jnp.where(y_at == 0, south, roll(here, EDGE))
        elif dy > 0:
            moved = jnp.where(y_at == EDGE - 1, north, roll(here, PLANE - EDGE))
        else:
            moved = here
        rims = []
        for near, edge in zip(nears, (1 - EDGE, EDGE - 1)):
            if near is None:
                rims.append(0.0)
                continue
            rim = roll(near, (edge - dy * EDGE) % PLANE)
            if dy < 0:
                rim = jnp.where(y_at == 0, 0.0, rim)
            elif dy > 0:
                rim = jnp.where(y_at == EDGE - 1, 0.0, rim)
            rims.append(rim)
        low = jnp.where(z_at == 0, rims[0], roll(moved, 1))
        high = jnp.where(z_at == EDGE - 1, rims[1], roll(moved, PLANE - 1))
        for dz, value in ((-1, low), (0, moved), (1, high)):
            tap = 3 * (dy + 1) + dz + 1
            taps[slot, pl.ds(tap * channels, channels), :] = value.astype(jnp.bfloat16)


def near_planes(cube, level, at):
    levels = cube.shape[0]
    return [
        cube[k, at].astype(jnp.float32) if 0 <= k < levels else None for k in (level - 1, level + 1)
    ]


def build_taps(level, cube, halo, taps, at, slot):
    at = jnp.asarray(at, jnp.int32)
    inner = ((at >= 1) & (at <= EDGE)).astype(jnp.float32)
    base = (at - 1) * EDGE
    west = (at == 0).astype(jnp.bfloat16)
    east = (at == EDGE + 1).astype(jnp.bfloat16)
    here = cube[level, at] + halo[0, level] * west + halo[1, level] * east
    south = halo[2, level].astype(jnp.float32) * inner
    north = halo[3, level].astype(jnp.float32) * inner
    south = pltpu.roll(south, (2 * PLANE - base) % PLANE, 1)
    north = pltpu.roll(north, (2 * PLANE - EDGE - base) % PLANE, 1)
    shift_nine(here.astype(jnp.float32), south, north, near_planes(cube, level, at), taps, slot)


def add_plane(w, live, level, taps, carry, ref, at, slot):
    channels = carry.shape[1]
    at = jnp.asarray(at, jnp.int32)
    target = pl.ds(pl.multiple_of(jnp.maximum(at - 2, 0) * PLANE, PLANE), PLANE)
    y = jnp.dot(w, taps[slot], preferred_element_type=jnp.float32)
    before, middle, after = (y[i * channels : (i + 1) * channels] for i in range(3))
    ref[level, :, target] = ((after + carry[0]) * live).astype(jnp.bfloat16)
    carry[0] = middle + carry[1]
    carry[1] = before


def run_pairs(first, end, build, multiply, base=0):
    def pair(i, unused):
        at = base + 2 * i
        build(at + 1, 1)
        multiply(at, 0)
        build(jnp.minimum(at + 2, EDGE + 1), 0)
        multiply(at + 1, 1)
        return unused

    lax.fori_loop(first, end, pair, 0)


def ahead_kernel(
    counts, scale, act_ref, f_ref, g_ref, gw_ref, halo_f, halo_g,
    send_f, send_g, cube, own, taps, gw, edges, f_sem, f_recv, g_sem, g_recv,
):
    levels, channels, _ = f_ref.shape
    depth = 9 * channels
    faces = side_faces(counts)
    barrier = pltpu.get_barrier_semaphore()
    for exists, target in faces:

        @pl.when(exists)
        def _():
            pl.semaphore_signal(barrier, inc=1, device_id=target, device_id_type=MESH)

    fill_faces(act_ref, f_ref, send_f)
    pl.semaphore_wait(barrier, sum(exists.astype(jnp.int32) for exists, _target in faces))
    send_faces(faces, send_f, halo_f, f_sem, f_recv)
    fill_faces(act_ref, g_ref, send_g)
    send_faces(faces, send_g, halo_g, g_sem, g_recv)

    lay_cube(act_ref, f_ref, cube)
    gw[...] = jnp.zeros_like(gw)
    zero = jnp.zeros((channels, PLANE), jnp.bfloat16)
    for level in range(levels):
        live = act_ref[0, level].astype(jnp.bfloat16)
        for at in (0, 1, EDGE + 2, EDGE + 3):
            own[level, at] = zero
        for x in range(EDGE):
            own[level, x + 2] = g_ref[level, :, x * PLANE : (x + 1) * PLANE] * live

    def product(left, slot):
        return lax.dot_general(
            left, taps[slot], (((1,), (1,)), ((), ())), preferred_element_type=jnp.float32
        )

    for level in range(levels):

        def build(at, slot):
            here = cube[level, at].astype(jnp.float32)
            shift_nine(here, 0.0, 0.0, near_planes(cube, level, at), taps, slot)

        def multiply(at, slot):
            gw[...] += product(own[level, pl.ds(at, 3)].reshape(3 * channels, PLANE), slot)

        build(1, 0)
        run_pairs(0, EDGE // 2, build, multiply, 1)

    await_faces(faces, send_f, halo_f, f_sem, f_recv)
    for level in range(levels):
        for slot, at in enumerate((0, EDGE + 1)):
            here = halo_f[slot, level].astype(jnp.float32)
            shift_nine(here, 0.0, 0.0, (None, None), taps, slot)
            gw[...] += product(own[level, pl.ds(at, 3)].reshape(3 * channels, PLANE), slot)
        for slot in range(2):
            here = halo_f[2 + slot, level].astype(jnp.float32)
            shift_nine(here, 0.0, 0.0, (None, None), taps, slot)
            term = product(send_g[2 + slot, level], slot)
            edges[slot] = edges[slot] + term if level else term

    third = depth // 3
    for dx in range(3):
        part = slice(dx * third, (dx + 1) * third)
        rows = gw[(2 - dx) * channels : (3 - dx) * channels, :]
        south = rows[:, :third] + edges[0][:, part]
        north = rows[:, 2 * third :] + edges[1][:, part]
        joined = jnp.concatenate([south, rows[:, third : 2 * third], north], axis=1)
        gw_ref[dx] = joined * scale
    await_faces(faces, send_g, halo_g, g_sem, g_recv)


def ahead(counts, scale, act, f, g):
    levels, channels, vox = f.shape
    depth = 9 * channels
    vmem = pl.BlockSpec(memory_space=pltpu.VMEM)
    halo = (4, levels, channels, PLANE)
    return pl.pallas_call(
        functools.partial(ahead_kernel, counts, scale),
        out_shape=(
            jax.ShapeDtypeStruct((3, channels, depth), jnp.float32),
            jax.ShapeDtypeStruct(halo, jnp.bfloat16),
            jax.ShapeDtypeStruct(halo, jnp.bfloat16),
        ),
        in_specs=[pl.BlockSpec(memory_space=pltpu.SMEM)] + [vmem] * 2,
        out_specs=(vmem,) * 3,
        scratch_shapes=[
            pltpu.VMEM(halo, jnp.bfloat16),
            pltpu.VMEM(halo, jnp.bfloat16),
            pltpu.VMEM((levels, EDGE + 2, channels, PLANE), jnp.bfloat16),
            pltpu.VMEM((levels, EDGE + 4, channels, PLANE), jnp.bfloat16),
            pltpu.VMEM((2, depth, PLANE), jnp.bfloat16),
            pltpu.VMEM((3 * channels, depth), jnp.float32),
            pltpu.VMEM((2, channels, depth), jnp.float32),
        ]
        + [pltpu.SemaphoreType.DMA((4,))] * 4,
        compiler_params=pltpu.CompilerParams(
            collective_id=0, has_side_effects=True, vmem_limit_bytes=48 << 20
        ),
        cost_estimate=pl.CostEstimate(
            flops=levels * 2 * 27 * channels * channels * vox,
            bytes_accessed=8 * levels * channels * vox,
            transcendentals=0,
        ),
    )(act, f, g)


def lay_weights(weight_ref, w):
    channels = weight_ref.shape[0]
    depth = 9 * channels
    wide = weight_ref[...].astype(jnp.float32)
    w[...] = jnp.zeros_like(w)
    for dx in range(3):
        rows = slice(dx * channels, (dx + 1) * channels)
        w[0, rows, :depth] = wide[:, dx * depth : (dx + 1) * depth].astype(jnp.bfloat16)
        blocks = []
        for tap in range(9):
            start = ((2 - dx) * 9 + 8 - tap) * channels
            blocks.append(wide[:, start : start + channels].T)
        w[1, rows, :depth] = jnp.concatenate(blocks, axis=1).astype(jnp.bfloat16)


def back_kernel(
    stages, act_ref, f_ref, g_ref, halo_f, halo_g, weight_ref, x_ref, out_ref, gin_ref, sum_ref,
    *scratch,
):
    count = len(stages)
    acc, recv = scratch[: max(count - 1, 0)], scratch[max(count - 1, 0) : -6]
    cube, taps, carry, w, send_sem, recv_sem = scratch[-6:]
    levels, channels, _ = g_ref.shape
    here = {axis: lax.axis_index(axis) for axis in AXES}
    partners = []
    for axis, step in stages:
        bit = here[axis] // step % 2
        partners.append((bit, {axis: here[axis] + step - 2 * step * bit}))
    if count:
        barrier = pltpu.get_barrier_semaphore()
        for _bit, partner in partners:
            pl.semaphore_signal(barrier, inc=1, device_id=partner, device_id_type=MESH)
    sources = (x_ref,) + tuple(acc)

    def copy_of(stage):
        bit, partner = partners[stage]
        half = sources[stage].shape[0] // 2
        return pltpu.make_async_remote_copy(
            src_ref=sources[stage].at[pl.ds((1 - bit) * half, half)],
            dst_ref=recv[stage],
            send_sem=send_sem.at[stage],
            recv_sem=recv_sem.at[stage],
            device_id=partner,
            device_id_type=MESH,
        )

    def finish(stage):
        copy_of(stage).wait()
        half = sources[stage].shape[0] // 2
        bit = partners[stage][0]
        total = sources[stage][pl.ds(bit * half, half)] + recv[stage][...]
        if stage + 1 < count:
            acc[stage][...] = total
            copy_of(stage + 1).start()
        else:
            sum_ref[...] = total

    if count:
        pl.semaphore_wait(barrier, count)
        copy_of(0).start()
    else:
        sum_ref[...] = x_ref[...]

    lay_weights(weight_ref, w)
    taps[...] = jnp.zeros_like(taps)
    lay_cube(act_ref, f_ref, cube.at[0])
    lay_cube(act_ref, g_ref, cube.at[1])
    pairs = EDGE // 2 + 1
    lengths = [1.2 + 5 * 0.5 ** (i - 1) if i else 2.0 for i in range(count)]
    stops = [round(0.8 * levels * pairs * sum(lengths[: i + 1]) / sum(lengths)) for i in range(count)]
    for level in range(levels):
        live = act_ref[0, level].astype(jnp.float32)
        carry[...] = jnp.zeros_like(carry)
        work = ((halo_f, out_ref), (halo_g, gin_ref))

        def build(at, slot):
            for k, (halo, _ref) in enumerate(work):
                build_taps(level, cube.at[k], halo, taps.at[k], at, slot)

        def multiply(at, slot):
            for k, (_halo, ref) in enumerate(work):
                add_plane(w[k], live, level, taps.at[k], carry.at[k], ref, at, slot)

        build(0, 0)
        at = 0
        for stage, stop in enumerate(stops):
            stop = stop - level * pairs
            if 0 < stop <= pairs:
                run_pairs(at, stop, build, multiply)
                at = stop
                finish(stage)
        if at < pairs:
            run_pairs(at, pairs, build, multiply)


def behind(stages, act, f, g, halo_f, halo_g, weight, parts):
    levels, channels, vox = g.shape
    full = 9 * channels + -9 * channels % 128
    vmem = pl.BlockSpec(memory_space=pltpu.VMEM)
    sizes = [parts.shape[0] >> (i + 1) for i in range(len(stages))]
    tail = parts.shape[1:]
    count = len(stages)
    return pl.pallas_call(
        functools.partial(back_kernel, stages),
        out_shape=(
            jax.ShapeDtypeStruct(f.shape, jnp.bfloat16),
            jax.ShapeDtypeStruct(g.shape, jnp.bfloat16),
            jax.ShapeDtypeStruct((parts.shape[0] >> count,) + tail, jnp.float32),
        ),
        in_specs=[pl.BlockSpec(memory_space=pltpu.SMEM)] + [vmem] * 6,
        out_specs=(vmem, vmem, vmem),
        scratch_shapes=[pltpu.VMEM((size,) + tail, jnp.float32) for size in sizes[:-1]]
        + [pltpu.VMEM((size,) + tail, jnp.float32) for size in sizes]
        + [
            pltpu.VMEM((2, levels, EDGE + 2, channels, PLANE), jnp.bfloat16),
            pltpu.VMEM((2, 2, full, PLANE), jnp.bfloat16),
            pltpu.VMEM((2, 2, channels, PLANE), jnp.float32),
            pltpu.VMEM((2, 3 * channels, full), jnp.bfloat16),
        ]
        + [pltpu.SemaphoreType.DMA((max(count, 1),))] * 2,
        compiler_params=pltpu.CompilerParams(
            collective_id=1 if count else None, has_side_effects=True, vmem_limit_bytes=48 << 20
        ),
        cost_estimate=pl.CostEstimate(
            flops=levels * 4 * 27 * channels * channels * vox,
            bytes_accessed=16 * levels * channels * vox,
            transcendentals=0,
        ),
    )(act, f, g, halo_f, halo_g, weight, parts)


def power_of_two(n):
    return n & (n - 1) == 0


def body(features, grad_out, weight, active):
    counts = [lax.axis_size(axis) for axis in AXES]
    levels, channels, vox = features.shape[2:]
    f, g, act = features[0, 0], grad_out[0, 0], active[0]
    scale = 1.0 / math.sqrt(counts[0] * counts[1] * levels * vox)
    gw, halo_f, halo_g = ahead(counts, scale, act, f, g)
    operands = (act, f, g, halo_f, halo_g, weight)
    flat = gw.transpose(1, 0, 2).reshape(-1)
    devices = counts[0] * counts[1]
    chunk = flat.shape[0] // devices
    if devices > 1 and all(map(power_of_two, counts)) and chunk % 8 == 0:
        bits = [count.bit_length() - 1 for count in counts]
        total = sum(bits)
        order = [bits[0] - 1 - i for i in range(bits[0])] + [total - 1 - i for i in range(bits[1])]
        parts = flat.reshape((2,) * total + (8, chunk // 8))
        parts = parts.transpose(order + [total, total + 1]).reshape(devices, 8, chunk // 8)
        stages = [(AXES[a], 1 << i) for a in range(2) for i in range(bits[a])]
        out, gin, summed = behind(stages, *operands, parts)
        summed = summed.reshape(chunk)
    else:
        out, gin, _ = behind([], *operands, jnp.zeros((1, 8, 128), jnp.float32))
        summed = lax.psum_scatter(flat, AXES, scatter_dimension=0, tiled=True)
    return out[None, None], gin[None, None], summed


def solution(mesh):
    placed = (P("gx", "gy", None, None, None), P("gx", "gy", None, None, None), P(), P("gx", "gy", None))
    return jax.shard_map(
        body,
        mesh=mesh,
        in_specs=placed,
        out_specs=(
            P("gx", "gy", None, None, None),
            P("gx", "gy", None, None, None),
            P(("gx", "gy")),
        ),
        check_vma=False,
    )
```
